32 devices in a mesh: groups: 2 (over y), row: 4 (over z), col: 2 (over x), tok: 2 (over core).
Axes of the slice: x: 2, y: 2, z: 4, core: 2. Of those that a mesh axis runs over, the one named last changes fastest.
Arguments:
- tokens: bfloat16 [512, 8192], P(('groups', 'row', 'tok'), 'col'), parts along dimension 0, may hold values from -12 to 12
- up_weight: bfloat16 [8192, 32768], P('col', ('row', 'tok')), may hold values from -0.5 to 0.5
- block_mask: int32 [64, 256], P('col', ('row', 'tok')), may hold values from 0 to 1, as said below
Outputs:
- column_rms: float32 [65536], P(('groups', 'row', 'tok')), parts along dimension 0
The draws below stay inside these ranges and needn't reach their ends.
There are 2 independent parts, one for each index of `groups`. The reference program is written for one: setup_inputs(seed, part) draws one part's arguments, and reference() takes and returns one part's arrays. A program takes and returns all parts, laid end to end along the dimension named above; an argument that names none is the same for every part. Nothing has to cross between parts.
Inputs may be any that keep to these rules, and one draw needn't show every extreme that they name: `block_mask`: in every block column, the block rows held by one index of col contain at most 24 ones, and some block column reaches 24; about half of all blocks are kept.
All inputs are finite; a program needn't handle non-finite values.
Results may differ from the reference program's by a relative error of at most 0.0003.
Values may be sent and summed in bfloat16 or wider, within the bound.
A program may use at most 256 MiB of HBM per device.

```python
import math
import jax
import jax.numpy as jnp
from jax import lax

D = 8192
FF = 32768
BLOCK = 128
TOKENS = 256
N_COL = 2


def draw_tokens(key, part):
    key = jax.random.fold_in(key, 11)
    key_base, key_rows = jax.random.split(key, 2)
    base = jax.random.normal(key_base, (TOKENS, D), jnp.float32)
    scales = jnp.exp(jax.random.uniform(key_rows, (TOKENS, 1), jnp.float32, math.log(0.3), math.log(3.0)))
    values = base * scales
    return jnp.clip(values, -12.0, 12.0).astype(jnp.bfloat16)


def draw_up_weight(key, part):
    key = jax.random.fold_in(key, 23)
    key_base, key_cols = jax.random.split(key, 2)
    fan_scale = (D * 0.5) ** (-0.5)
    base = jax.random.normal(key_base, (D, FF), jnp.float32)
    scales = jnp.exp(jax.random.uniform(key_cols, (1, FF), jnp.float32, math.log(0.3), math.log(3.0)))
    return jnp.clip(base * scales * fan_scale, -0.5, 0.5).astype(jnp.bfloat16)


def draw_block_mask(key, part):
    key = jax.random.fold_in(key, 37)
    key_counts, key_forced, key_bits = jax.random.split(key, 3)
    tile_rows = D // (BLOCK * N_COL)
    block_cols = FF // BLOCK
    most_kept = 3 * tile_rows // 4
    counts_kept = jax.random.randint(key_counts, (N_COL, block_cols), tile_rows // 4, most_kept + 1)
    forced_at = jax.random.randint(key_forced, (), 0, N_COL * block_cols)
    flat_index = jnp.arange(N_COL * block_cols, dtype=jnp.int32).reshape(N_COL, block_cols)
    counts_kept = jnp.where(flat_index == forced_at, most_kept, counts_kept)
    random_bits = jax.random.randint(key_bits, (N_COL, block_cols, tile_rows), 0, 2 ** 20) * tile_rows
    random_bits = random_bits + jnp.arange(tile_rows, dtype=jnp.int32)[None, None, :]
    ranking = jnp.argsort(jnp.argsort(random_bits, axis=-1), axis=-1)
    keep_mask = (ranking < counts_kept[:, :, None]).astype(jnp.int32)
    keep_mask = jnp.transpose(keep_mask, (0, 2, 1)).reshape(N_COL * tile_rows, block_cols)
    return keep_mask


def setup_inputs(seed: int = 0, part: int = 0) -> dict:
    key_list = jax.random.split(jax.random.key(seed), 4)
    part_keys = jax.random.split(jax.random.fold_in(key_list[3], part), 4)
    tokens = draw_tokens(jax.random.fold_in(jax.random.fold_in(key_list[3], part), 71), part)
    up_weight = draw_up_weight(jax.random.fold_in(key_list[3], 71), part)
    block_mask = draw_block_mask(jax.random.fold_in(key_list[3], 71), part)
    return dict(tokens=tokens, up_weight=up_weight, block_mask=block_mask)


def reference(tokens, up_weight, block_mask):
    keep_mask = jnp.repeat(jnp.repeat(block_mask > 0, BLOCK, axis=0), BLOCK, axis=1)
    masked = jnp.where(keep_mask, up_weight, jnp.zeros_like(up_weight))
    pre = jnp.dot(tokens, masked, preferred_element_type=jnp.float32)
    activated = jax.nn.gelu(pre, approximate=False)
    totals = lax.optimization_barrier(jnp.sum(activated * activated, axis=0))
    return jnp.sqrt(totals / TOKENS + 1e-06)
```

```python
import functools

import jax
import jax.numpy as jnp
from jax import lax
from jax.experimental import pallas as pl
from jax.experimental.pallas import tpu as pltpu
from jax.sharding import PartitionSpec as P

BLOCK = 128
TILE = 512
VMEM_CAP = 40 * 2**20
MESH = pl.DeviceIdType.MESH


def per_device(tokens, up_weight, block_mask):
    keep_mask = jnp.repeat(jnp.repeat(block_mask > 0, BLOCK, axis=0), BLOCK, axis=1)
    masked = jnp.where(keep_mask, up_weight, jnp.zeros_like(up_weight))
    partial_value = jnp.dot(
        lax.all_gather(tokens, ("row", "tok"), axis=0, tiled=True),
        masked,
        preferred_element_type=jnp.float32,
    )
    token_count = partial_value.shape[0]
    shares = lax.psum_scatter(partial_value, "col", scatter_dimension=0, tiled=True)
    activated = jax.nn.gelu(shares, approximate=False)
    local_sums = jnp.sum(activated * activated, axis=0)
    totals = lax.psum(local_sums, "col")
    return jnp.sqrt(totals / token_count + 1e-06)


def kernel(
    rows, tile, tok_ref, w_hbm, mask_ref, out_ref,
    w, toks, own, sent, sent_scale, got, got_scale, sums, sums_got,
    w_sem, z_send, z_recv, p_send, p_recv, x_send, x_recv, s_send, s_recv, t_send, t_recv,
):
    r = lax.axis_index("row")
    c = lax.axis_index("col")
    k = lax.axis_index("tok")
    held, depth = tok_ref.shape
    width = w_hbm.shape[1]
    tiles = width // tile
    units = rows * tiles

    def load(j):
        return pltpu.make_async_copy(
            w_hbm.at[:, pl.ds(pl.multiple_of(j * tile, tile), tile)], w.at[j], w_sem.at[j]
        )

    @pl.loop(0, tiles)
    def _(j):
        load(j).start()

    barrier = pltpu.get_barrier_semaphore()
    pl.semaphore_signal(barrier, inc=1, device_id={"tok": 1 - k}, device_id_type=MESH)
    pl.semaphore_signal(barrier, inc=1, device_id={"col": 1 - c}, device_id_type=MESH)

    @pl.when(r > 0)
    def _():
        pl.semaphore_signal(barrier, inc=1, device_id={"row": r - 1}, device_id_type=MESH)

    @pl.when(r < rows - 1)
    def _():
        pl.semaphore_signal(barrier, inc=1, device_id={"row": r + 1}, device_id_type=MESH)

    pl.semaphore_wait(barrier, 2 + jnp.minimum(r, 1) + jnp.minimum(rows - 1 - r, 1))

    def along(s, direction, from_input=False):
        return pltpu.make_async_remote_copy(
            src_ref=tok_ref if from_input else toks.at[s, k],
            dst_ref=toks.at[s, k],
            send_sem=z_send.at[direction, s],
            recv_sem=z_recv.at[s],
            device_id={"row": r + 2 * direction - 1},
            device_id_type=MESH,
        )

    def across(s, from_input=False):
        return pltpu.make_async_remote_copy(
            src_ref=tok_ref if from_input else toks.at[s, k],
            dst_ref=toks.at[s, k],
            send_sem=p_send.at[s],
            recv_sem=p_recv.at[s],
            device_id={"tok": 1 - k},
            device_id_type=MESH,
        )

    def partials(u):
        return pltpu.make_async_remote_copy(
            src_ref=sent.at[u],
            dst_ref=got.at[u],
            send_sem=x_send.at[u],
            recv_sem=x_recv.at[u],
            device_id={"col": 1 - c},
            device_id_type=MESH,
        )

    def scales(u):
        return pltpu.make_async_remote_copy(
            src_ref=sent_scale.at[u],
            dst_ref=got_scale.at[u],
            send_sem=s_send.at[u],
            recv_sem=s_recv.at[u],
            device_id={"col": 1 - c},
            device_id_type=MESH,
        )

    across(r, True).start()

    @pl.when(r > 0)
    def _():
        along(r, 0, True).start()

    @pl.when(r < rows - 1)
    def _():
        along(r, 1, True).start()

    toks[r, k] = tok_ref[...]
    sums[...] = jnp.zeros_like(sums)

    def forward(d):
        @pl.when(r - d >= 0)
        def _():
            s = r - d
            along(s, 1).wait_recv()

            @pl.when(r < rows - 1)
            def _():
                along(s, 1).start()

            across(s).start()

        @pl.when(r + d < rows)
        def _():
            s = r + d
            along(s, 0).wait_recv()

            @pl.when(r > 0)
            def _():
                along(s, 0).start()

            across(s).start()

    near = jnp.minimum(r, rows - 1 - r)

    def source(p):
        d = (p + 1) // 2
        paired = jnp.where(p % 2 == 1, r - d, r + d)
        return jnp.where(p <= 2 * near, paired, jnp.where(2 * r < rows - 1, p, rows - 1 - p))

    def finish(u):
        j = u % tiles
        partials(u).wait_recv()
        scales(u).wait_recv()
        theirs = got[u].astype(jnp.int32).astype(jnp.float32) * got_scale[u]
        v = own[u] + theirs
        a = 0.5 * v * (1.0 + lax.erf(v * (0.5**0.5)))
        sums[j] += jnp.sum(a * a, axis=0, keepdims=True)

    def unit(u, carry):
        p = u // tiles
        j = u % tiles
        s = source(p)

        @pl.when(p == 0)
        def _():
            load(j).wait()

            @pl.loop(0, depth // BLOCK)
            def _(i):
                at = pl.ds(pl.multiple_of(i * BLOCK, BLOCK), BLOCK)
                for b in range(tile // BLOCK):
                    keep = (mask_ref[i, j * (tile // BLOCK) + b] > 0).astype(jnp.float32)
                    cols = slice(b * BLOCK, (b + 1) * BLOCK)
                    w[j, at, cols] = w[j, at, cols] * jnp.full((BLOCK, BLOCK), keep).astype(jnp.bfloat16)

        @pl.when(jnp.logical_and(j == tiles // 2, p < rows - 1))
        def _():
            forward(p + 1)

        @pl.when(j == 0)
        def _():
            across(s).wait_recv()

        pre = jnp.dot(
            toks[s].reshape(2 * held, depth), w[j], preferred_element_type=jnp.float32
        )
        own[u] = jnp.where(c == 0, pre[:held], pre[held:])
        other = jnp.where(c == 0, pre[held:], pre[:held])
        top = jnp.maximum(jnp.max(jnp.abs(other), axis=0, keepdims=True), 1e-30)
        sent_scale[u] = top * (1.0 / 32766.0)
        sent[u] = jnp.round(other * (32766.0 / top)).astype(jnp.int32).astype(jnp.int16)
        partials(u).start()
        scales(u).start()

        @pl.when(u >= tiles)
        def _():
            finish(u - tiles)

        return carry

    lax.fori_loop(0, units, unit, 0)

    @pl.loop(units - tiles, units)
    def _(u):
        finish(u)

    total = pltpu.make_async_remote_copy(
        src_ref=sums,
        dst_ref=sums_got,
        send_sem=t_send,
        recv_sem=t_recv,
        device_id={"col": 1 - c},
        device_id_type=MESH,
    )
    total.start()

    @pl.loop(0, units)
    def _(u):
        partials(u).wait_send()
        scales(u).wait_send()

    @pl.loop(0, rows)
    def _(s):
        across(s).wait_send()

        @pl.when(jnp.logical_and(s <= r, r < rows - 1))
        def _():
            along(s, 1).wait_send()

        @pl.when(jnp.logical_and(s >= r, r > 0))
        def _():
            along(s, 0).wait_send()

    total.wait()
    count = rows * 2 * held
    out_ref[...] = jnp.sqrt((sums[...] + sums_got[...]) / count + 1e-06)


def fused(rows, tokens, up_weight, block_mask):
    held, depth = tokens.shape
    width = up_weight.shape[1]
    tile = min(TILE, width)
    tiles = width // tile
    units = rows * tiles
    dma = pltpu.SemaphoreType.DMA
    out = pl.pallas_call(
        functools.partial(kernel, rows, tile),
        out_shape=jax.ShapeDtypeStruct((tiles, 1, tile), jnp.float32),
        in_specs=[
            pl.BlockSpec(memory_space=pltpu.VMEM),
            pl.BlockSpec(memory_space=pl.ANY),
            pl.BlockSpec(memory_space=pltpu.SMEM),
        ],
        out_specs=pl.BlockSpec(memory_space=pltpu.VMEM),
        scratch_shapes=[
            pltpu.VMEM((tiles, depth, tile), jnp.bfloat16),
            pltpu.VMEM((rows, 2, held, depth), jnp.bfloat16),
            pltpu.VMEM((units, held, tile), jnp.float32),
            pltpu.VMEM((units, held, tile), jnp.int16),
            pltpu.VMEM((units, 1, tile), jnp.float32),
            pltpu.VMEM((units, held, tile), jnp.int16),
            pltpu.VMEM((units, 1, tile), jnp.float32),
            pltpu.VMEM((tiles, 1, tile), jnp.float32),
            pltpu.VMEM((tiles, 1, tile), jnp.float32),
            dma((tiles,)),
            dma((2, rows)),
            dma((rows,)),
            dma((rows,)),
            dma((rows,)),
            dma((units,)),
            dma((units,)),
            dma((units,)),
            dma((units,)),
            dma,
            dma,
        ],
        compiler_params=pltpu.CompilerParams(
            collective_id=0, has_side_effects=True, vmem_limit_bytes=56 * 2**20
        ),
    )(tokens, up_weight, block_mask)
    return out.reshape(width)


def solution(mesh):
    placed = (
        P(("groups", "row", "tok"), "col"),
        P("col", ("row", "tok")),
        P("col", ("row", "tok")),
    )
    rows = mesh.shape["row"]
    pairs = mesh.shape["col"] == 2 and mesh.shape["tok"] == 2 and rows > 1

    def body(tokens, up_weight, block_mask):
        held, depth = tokens.shape
        width = up_weight.shape[1]
        fits = up_weight.size * 2 <= VMEM_CAP and held % 16 == 0
        fits = fits and depth % BLOCK == 0 and width % min(TILE, width) == 0
        if pairs and fits:
            return fused(rows, tokens, up_weight, block_mask)
        return per_device(tokens, up_weight, block_mask)

    return jax.shard_map(
        body,
        mesh=mesh,
        in_specs=placed,
        out_specs=P(("groups", "row", "tok")),
        check_vma=False,
    )
```

```python
import functools

import jax
import jax.numpy as jnp
from jax import lax
from jax.experimental import pallas as pl
from jax.experimental.pallas import tpu as pltpu
from jax.sharding import PartitionSpec as P

BLOCK = 128
TILE = 512
EARLY = 4
VMEM_CAP = 40 * 2**20
MESH = pl.DeviceIdType.MESH


def per_device(tokens, up_weight, block_mask):
    keep_mask = jnp.repeat(jnp.repeat(block_mask > 0, BLOCK, axis=0), BLOCK, axis=1)
    masked = jnp.where(keep_mask, up_weight, jnp.zeros_like(up_weight))
    partial_value = jnp.dot(
        lax.all_gather(tokens, ("row", "tok"), axis=0, tiled=True),
        masked,
        preferred_element_type=jnp.float32,
    )
    token_count = partial_value.shape[0]
    shares = lax.psum_scatter(partial_value, "col", scatter_dimension=0, tiled=True)
    activated = jax.nn.gelu(shares, approximate=False)
    local_sums = jnp.sum(activated * activated, axis=0)
    totals = lax.psum(local_sums, "col")
    return jnp.sqrt(totals / token_count + 1e-06)


def kernel(
    rows, tile, tok_ref, w_hbm, mask_ref, out_ref,
    w, toks, own, sent, sent_scale, got, got_scale, sums, sums_got,
    w_sem, z_send, z_recv, p_send, p_recv, x_send, x_recv, s_send, s_recv, t_send, t_recv,
):
    r = lax.axis_index("row")
    c = lax.axis_index("col")
    k = lax.axis_index("tok")
    held, depth = tok_ref.shape
    width = w_hbm.shape[1]
    tiles = width // tile
    units = rows * tiles
    early = min(EARLY, tiles)

    def load(j):
        return pltpu.make_async_copy(
            w_hbm.at[:, pl.ds(pl.multiple_of(j * tile, tile), tile)], w.at[j], w_sem.at[j]
        )

    @pl.loop(0, tiles)
    def _(j):
        load(j).start()

    barrier = pltpu.get_barrier_semaphore()
    pl.semaphore_signal(barrier, inc=1, device_id={"tok": 1 - k}, device_id_type=MESH)
    pl.semaphore_signal(barrier, inc=1, device_id={"col": 1 - c}, device_id_type=MESH)

    @pl.when(r > 0)
    def _():
        pl.semaphore_signal(barrier, inc=1, device_id={"row": r - 1}, device_id_type=MESH)

    @pl.when(r < rows - 1)
    def _():
        pl.semaphore_signal(barrier, inc=1, device_id={"row": r + 1}, device_id_type=MESH)

    pl.semaphore_wait(barrier, 2 + jnp.minimum(r, 1) + jnp.minimum(rows - 1 - r, 1))

    def along(s, direction, from_input=False):
        return pltpu.make_async_remote_copy(
            src_ref=tok_ref if from_input else toks.at[s, k],
            dst_ref=toks.at[s, k],
            send_sem=z_send.at[direction, s],
            recv_sem=z_recv.at[s],
            device_id={"row": r + 2 * direction - 1},
            device_id_type=MESH,
        )

    def across(s, from_input=False):
        return pltpu.make_async_remote_copy(
            src_ref=tok_ref if from_input else toks.at[s, k],
            dst_ref=toks.at[s, k],
            send_sem=p_send.at[s],
            recv_sem=p_recv.at[s],
            device_id={"tok": 1 - k},
            device_id_type=MESH,
        )

    def partials(u):
        return pltpu.make_async_remote_copy(
            src_ref=sent.at[u],
            dst_ref=got.at[u],
            send_sem=x_send.at[u],
            recv_sem=x_recv.at[u],
            device_id={"col": 1 - c},
            device_id_type=MESH,
        )

    def scales(u):
        return pltpu.make_async_remote_copy(
            src_ref=sent_scale.at[u],
            dst_ref=got_scale.at[u],
            send_sem=s_send.at[u],
            recv_sem=s_recv.at[u],
            device_id={"col": 1 - c},
            device_id_type=MESH,
        )

    across(r, True).start()

    @pl.when(r > 0)
    def _():
        along(r, 0, True).start()

    @pl.when(r < rows - 1)
    def _():
        along(r, 1, True).start()

    toks[r, k] = tok_ref[...]
    sums[...] = jnp.zeros_like(sums)

    def forward(d):
        @pl.when(r - d >= 0)
        def _():
            s = r - d
            along(s, 1).wait_recv()

            @pl.when(r < rows - 1)
            def _():
                along(s, 1).start()

            across(s).start()

        @pl.when(r + d < rows)
        def _():
            s = r + d
            along(s, 0).wait_recv()

            @pl.when(r > 0)
            def _():
                along(s, 0).start()

            across(s).start()

    near = jnp.minimum(r, rows - 1 - r)

    def source(p):
        d = (p + 1) // 2
        paired = jnp.where(p % 2 == 1, r - d, r + d)
        return jnp.where(p <= 2 * near, paired, jnp.where(2 * r < rows - 1, p, rows - 1 - p))

    def finish(u):
        j = u % tiles
        partials(u).wait_recv()
        scales(u).wait_recv()
        theirs = got[u].astype(jnp.int32).astype(jnp.float32) * got_scale[u]
        v = own[u] + theirs
        a = 0.5 * v * (1.0 + lax.erf(v * (0.5**0.5)))
        sums[j] += jnp.sum(a * a, axis=0, keepdims=True)

    def dot(x, j):
        total = None
        for i in range(0, depth // BLOCK, 2):
            blocks = []
            for h in range(i, i + 2):
                line = []
                for b in range(tile // BLOCK):
                    keep = (mask_ref[h, j * (tile // BLOCK) + b] > 0).astype(jnp.float32)
                    keep = jnp.full((BLOCK, BLOCK), keep).astype(jnp.bfloat16)
                    line.append(
                        w[j, h * BLOCK : (h + 1) * BLOCK, b * BLOCK : (b + 1) * BLOCK] * keep
                    )
                blocks.append(jnp.concatenate(line, axis=1))
            part = jnp.dot(
                x[:, i * BLOCK : (i + 2) * BLOCK],
                jnp.concatenate(blocks, axis=0),
                preferred_element_type=jnp.float32,
            )
            total = part if total is None else total + part
        return total

    def emit(u, pre):
        own[u] = jnp.where(c == 0, pre[:held], pre[held:])
        other = jnp.where(c == 0, pre[held:], pre[:held])
        top = jnp.maximum(jnp.max(jnp.abs(other), axis=0, keepdims=True), 1e-30)
        sent_scale[u] = top * (1.0 / 32766.0)
        sent[u] = jnp.round(other * (32766.0 / top)).astype(jnp.int32).astype(jnp.int16)
        partials(u).start()
        scales(u).start()

    def chunk(p):
        return toks[source(p)].reshape(2 * held, depth)

    def single(p, j):
        emit(p * tiles + j, dot(chunk(p), j))

        @pl.when(p >= 2)
        def _():
            finish((p - 2) * tiles + j)

    def double(p, j):
        pre = dot(jnp.concatenate([chunk(p), chunk(p + 1)], axis=0), j)
        emit(p * tiles + j, pre[: 2 * held])
        emit((p + 1) * tiles + j, pre[2 * held :])

        @pl.when(p >= 2)
        def _():
            finish((p - 2) * tiles + j)
            finish((p - 1) * tiles + j)

    @pl.loop(0, rows // 2)
    def _(q):
        p = 2 * q
        across(source(p)).wait_recv()

        @pl.loop(0, early)
        def _(j):
            @pl.when(q == 0)
            def _():
                load(j).wait()

            single(p, j)

        forward(p + 1)
        across(source(p + 1)).wait_recv()

        @pl.loop(early, tiles)
        def _(j):
            @pl.when(q == 0)
            def _():
                load(j).wait()

            double(p, j)

        @pl.loop(0, early)
        def _(j):
            @pl.when(jnp.logical_and(j == early // 2, p + 2 < rows))
            def _():
                forward(p + 2)

            single(p + 1, j)

    @pl.loop(0, early)
    def _(j):
        finish((rows - 2) * tiles + j)

    @pl.loop(early, tiles)
    def _(j):
        finish((rows - 2) * tiles + j)
        finish((rows - 1) * tiles + j)

    @pl.loop(0, early)
    def _(j):
        finish((rows - 1) * tiles + j)

    total = pltpu.make_async_remote_copy(
        src_ref=sums,
        dst_ref=sums_got,
        send_sem=t_send,
        recv_sem=t_recv,
        device_id={"col": 1 - c},
        device_id_type=MESH,
    )
    total.start()

    @pl.loop(0, units)
    def _(u):
        partials(u).wait_send()
        scales(u).wait_send()

    @pl.loop(0, rows)
    def _(s):
        across(s).wait_send()

        @pl.when(jnp.logical_and(s <= r, r < rows - 1))
        def _():
            along(s, 1).wait_send()

        @pl.when(jnp.logical_and(s >= r, r > 0))
        def _():
            along(s, 0).wait_send()

    total.wait()
    count = rows * 2 * held
    out_ref[...] = jnp.sqrt((sums[...] + sums_got[...]) / count + 1e-06)


def fused(rows, tokens, up_weight, block_mask):
    held, depth = tokens.shape
    width = up_weight.shape[1]
    tile = min(TILE, width)
    tiles = width // tile
    units = rows * tiles
    dma = pltpu.SemaphoreType.DMA
    out = pl.pallas_call(
        functools.partial(kernel, rows, tile),
        out_shape=jax.ShapeDtypeStruct((tiles, 1, tile), jnp.float32),
        in_specs=[
            pl.BlockSpec(memory_space=pltpu.VMEM),
            pl.BlockSpec(memory_space=pl.ANY),
            pl.BlockSpec(memory_space=pltpu.SMEM),
        ],
        out_specs=pl.BlockSpec(memory_space=pltpu.VMEM),
        scratch_shapes=[
            pltpu.VMEM((tiles, depth, tile), jnp.bfloat16),
            pltpu.VMEM((rows, 2, held, depth), jnp.bfloat16),
            pltpu.VMEM((units, held, tile), jnp.float32),
            pltpu.VMEM((units, held, tile), jnp.int16),
            pltpu.VMEM((units, 1, tile), jnp.float32),
            pltpu.VMEM((units, held, tile), jnp.int16),
            pltpu.VMEM((units, 1, tile), jnp.float32),
            pltpu.VMEM((tiles, 1, tile), jnp.float32),
            pltpu.VMEM((tiles, 1, tile), jnp.float32),
            dma((tiles,)),
            dma((2, rows)),
            dma((rows,)),
            dma((rows,)),
            dma((rows,)),
            dma((units,)),
            dma((units,)),
            dma((units,)),
            dma((units,)),
            dma,
            dma,
        ],
        compiler_params=pltpu.CompilerParams(
            collective_id=0, has_side_effects=True, vmem_limit_bytes=56 * 2**20
        ),
    )(tokens, up_weight, block_mask)
    return out.reshape(width)


def solution(mesh):
    placed = (
        P(("groups", "row", "tok"), "col"),
        P("col", ("row", "tok")),
        P("col", ("row", "tok")),
    )
    rows = mesh.shape["row"]
    pairs = mesh.shape["col"] == 2 and mesh.shape["tok"] == 2 and rows % 2 == 0

    def body(tokens, up_weight, block_mask):
        held, depth = tokens.shape
        width = up_weight.shape[1]
        fits = up_weight.size * 2 <= VMEM_CAP and held % 16 == 0
        fits = fits and depth % (2 * BLOCK) == 0 and width % min(TILE, width) == 0
        if pairs and fits:
            return fused(rows, tokens, up_weight, block_mask)
        return per_device(tokens, up_weight, block_mask)

    return jax.shard_map(
        body,
        mesh=mesh,
        in_specs=placed,
        out_specs=P(("groups", "row", "tok")),
        check_vma=False,
    )
```

```python
import functools

import jax
import jax.numpy as jnp
from jax import lax
from jax.experimental import pallas as pl
from jax.experimental.pallas import tpu as pltpu
from jax.sharding import PartitionSpec as P

BLOCK = 128
TILE = 512
EARLY = 4
VMEM_CAP = 40 * 2**20
MESH = pl.DeviceIdType.MESH


def per_device(tokens, up_weight, block_mask):
    keep_mask = jnp.repeat(jnp.repeat(block_mask > 0, BLOCK, axis=0), BLOCK, axis=1)
    masked = jnp.where(keep_mask, up_weight, jnp.zeros_like(up_weight))
    partial_value = jnp.dot(
        lax.all_gather(tokens, ("row", "tok"), axis=0, tiled=True),
        masked,
        preferred_element_type=jnp.float32,
    )
    token_count = partial_value.shape[0]
    shares = lax.psum_scatter(partial_value, "col", scatter_dimension=0, tiled=True)
    activated = jax.nn.gelu(shares, approximate=False)
    local_sums = jnp.sum(activated * activated, axis=0)
    totals = lax.psum(local_sums, "col")
    return jnp.sqrt(totals / token_count + 1e-06)


def kernel(
    rows, tile, tok_ref, w_hbm, mask_ref, out_ref,
    w, toks, own, sent, sent_scale, got, got_scale, sums, sums_got,
    w_sem, z_send, z_recv, p_send, p_recv, x_send, x_recv, s_send, s_recv, t_send, t_recv,
):
    r = lax.axis_index("row")
    c = lax.axis_index("col")
    k = lax.axis_index("tok")
    held, depth = tok_ref.shape
    width = w_hbm.shape[1]
    tiles = width // tile
    units = rows * tiles
    early = min(EARLY, tiles - 1)

    def load(j):
        return pltpu.make_async_copy(
            w_hbm.at[:, pl.ds(pl.multiple_of(j * tile, tile), tile)], w.at[j], w_sem.at[j]
        )

    @pl.loop(0, tiles)
    def _(j):
        load(j).start()

    barrier = pltpu.get_barrier_semaphore()
    pl.semaphore_signal(barrier, inc=1, device_id={"tok": 1 - k}, device_id_type=MESH)
    pl.semaphore_signal(barrier, inc=1, device_id={"col": 1 - c}, device_id_type=MESH)

    @pl.when(r > 0)
    def _():
        pl.semaphore_signal(barrier, inc=1, device_id={"row": r - 1}, device_id_type=MESH)

    @pl.when(r < rows - 1)
    def _():
        pl.semaphore_signal(barrier, inc=1, device_id={"row": r + 1}, device_id_type=MESH)

    pl.semaphore_wait(barrier, 2 + jnp.minimum(r, 1) + jnp.minimum(rows - 1 - r, 1))

    def half(h):
        return slice(h * (depth // 2), (h + 1) * (depth // 2))

    def along(s, direction, h, from_input=False):
        return pltpu.make_async_remote_copy(
            src_ref=tok_ref.at[:, half(h)] if from_input else toks.at[s, k, :, half(h)],
            dst_ref=toks.at[s, k, :, half(h)],
            send_sem=z_send.at[direction, h, s],
            recv_sem=z_recv.at[h, s],
            device_id={"row": r + 2 * direction - 1},
            device_id_type=MESH,
        )

    def across(s, h, from_input=False):
        return pltpu.make_async_remote_copy(
            src_ref=tok_ref.at[:, half(h)] if from_input else toks.at[s, k, :, half(h)],
            dst_ref=toks.at[s, k, :, half(h)],
            send_sem=p_send.at[h, s],
            recv_sem=p_recv.at[h, s],
            device_id={"tok": 1 - k},
            device_id_type=MESH,
        )

    def partials(u):
        return pltpu.make_async_remote_copy(
            src_ref=sent.at[u],
            dst_ref=got.at[u],
            send_sem=x_send.at[u],
            recv_sem=x_recv.at[u],
            device_id={"col": 1 - c},
            device_id_type=MESH,
        )

    def scales(u):
        return pltpu.make_async_remote_copy(
            src_ref=sent_scale.at[u],
            dst_ref=got_scale.at[u],
            send_sem=s_send.at[u],
            recv_sem=s_recv.at[u],
            device_id={"col": 1 - c},
            device_id_type=MESH,
        )

    for h in range(2):
        across(r, h, True).start()

    @pl.when(r > 0)
    def _():
        for h in range(2):
            along(r, 0, h, True).start()

    @pl.when(r < rows - 1)
    def _():
        for h in range(2):
            along(r, 1, h, True).start()

    toks[r, k] = tok_ref[...]
    sums[...] = jnp.zeros_like(sums)

    def forward(d, h):
        @pl.when(r - d >= 0)
        def _():
            s = r - d
            along(s, 1, h).wait_recv()

            @pl.when(r < rows - 1)
            def _():
                along(s, 1, h).start()

            across(s, h).start()

        @pl.when(r + d < rows)
        def _():
            s = r + d
            along(s, 0, h).wait_recv()

            @pl.when(r > 0)
            def _():
                along(s, 0, h).start()

            across(s, h).start()

    near = jnp.minimum(r, rows - 1 - r)

    def source(p):
        d = (p + 1) // 2
        paired = jnp.where(p % 2 == 1, r - d, r + d)
        return jnp.where(p <= 2 * near, paired, jnp.where(2 * r < rows - 1, p, rows - 1 - p))

    def finish(u):
        j = u % tiles
        partials(u).wait_recv()
        scales(u).wait_recv()
        theirs = got[u].astype(jnp.int32).astype(jnp.float32) * got_scale[u]
        v = own[u] + theirs
        a = 0.5 * v * (1.0 + lax.erf(v * (0.5**0.5)))
        sums[j] += jnp.sum(a * a, axis=0, keepdims=True)

    def dot(x, j):
        total = None
        for i in range(0, depth // BLOCK, 2):
            blocks = []
            for h in range(i, i + 2):
                line = []
                for b in range(tile // BLOCK):
                    keep = (mask_ref[h, j * (tile // BLOCK) + b] > 0).astype(jnp.float32)
                    keep = jnp.full((BLOCK, BLOCK), keep).astype(jnp.bfloat16)
                    line.append(
                        w[j, h * BLOCK : (h + 1) * BLOCK, b * BLOCK : (b + 1) * BLOCK] * keep
                    )
                blocks.append(jnp.concatenate(line, axis=1))
            part = jnp.dot(
                x[:, i * BLOCK : (i + 2) * BLOCK],
                jnp.concatenate(blocks, axis=0),
                preferred_element_type=jnp.float32,
            )
            total = part if total is None else total + part
        return total

    def emit(u, pre):
        own[u] = jnp.where(c == 0, pre[:held], pre[held:])
        other = jnp.where(c == 0, pre[held:], pre[:held])
        top = jnp.maximum(jnp.max(jnp.abs(other), axis=0, keepdims=True), 1e-30)
        sent_scale[u] = top * (1.0 / 32766.0)
        sent[u] = jnp.round(other * (32766.0 / top)).astype(jnp.int32).astype(jnp.int16)
        partials(u).start()
        scales(u).start()

    def chunk(p):
        return toks[source(p)].reshape(2 * held, depth)

    def arrive(p):
        for h in range(2):
            across(source(p), h).wait_recv()

    def double(p, j):
        pre = dot(jnp.concatenate([chunk(p), chunk(p + 1)], axis=0), j)
        emit(p * tiles + j, pre[: 2 * held])
        emit((p + 1) * tiles + j, pre[2 * held :])

    arrive(0)

    @pl.loop(0, early)
    def _(j):
        load(j).wait()
        emit(j, dot(chunk(0), j))

    forward(1, 0)

    @pl.loop(0, rows - 1)
    def _(p):
        forward(p + 1, 1)
        arrive(p + 1)
        low = jnp.where(p % 2 == 0, early, 0)
        high = jnp.where(p % 2 == 0, tiles, early)

        @pl.loop(low, high)
        def _(j):
            @pl.when(p == 0)
            def _():
                load(j).wait()

            @pl.when(jnp.logical_and(j == high - 1, p + 2 < rows))
            def _():
                forward(p + 2, 0)

            double(p, j)

            @pl.when(p >= 2)
            def _():
                finish((p - 2) * tiles + j)

            @pl.when(p >= 1)
            def _():
                finish((p - 1) * tiles + j)

    @pl.loop(0, early)
    def _(j):
        emit((rows - 1) * tiles + j, dot(chunk(rows - 1), j))
        finish((rows - 3) * tiles + j)
        finish((rows - 2) * tiles + j)

    @pl.loop(early, tiles)
    def _(j):
        finish((rows - 2) * tiles + j)
        finish((rows - 1) * tiles + j)

    @pl.loop(0, early)
    def _(j):
        finish((rows - 1) * tiles + j)

    total = pltpu.make_async_remote_copy(
        src_ref=sums,
        dst_ref=sums_got,
        send_sem=t_send,
        recv_sem=t_recv,
        device_id={"col": 1 - c},
        device_id_type=MESH,
    )
    total.start()

    @pl.loop(0, units)
    def _(u):
        partials(u).wait_send()
        scales(u).wait_send()

    @pl.loop(0, rows)
    def _(s):
        for h in range(2):
            across(s, h).wait_send()

        @pl.when(jnp.logical_and(s <= r, r < rows - 1))
        def _():
            for h in range(2):
                along(s, 1, h).wait_send()

        @pl.when(jnp.logical_and(s >= r, r > 0))
        def _():
            for h in range(2):
                along(s, 0, h).wait_send()

    total.wait()
    count = rows * 2 * held
    out_ref[...] = jnp.sqrt((sums[...] + sums_got[...]) / count + 1e-06)


def fused(rows, tokens, up_weight, block_mask):
    held, depth = tokens.shape
    width = up_weight.shape[1]
    tile = TILE
    tiles = width // tile
    units = rows * tiles
    dma = pltpu.SemaphoreType.DMA
    out = pl.pallas_call(
        functools.partial(kernel, rows, tile),
        out_shape=jax.ShapeDtypeStruct((tiles, 1, tile), jnp.float32),
        in_specs=[
            pl.BlockSpec(memory_space=pltpu.VMEM),
            pl.BlockSpec(memory_space=pl.ANY),
            pl.BlockSpec(memory_space=pltpu.SMEM),
        ],
        out_specs=pl.BlockSpec(memory_space=pltpu.VMEM),
        scratch_shapes=[
            pltpu.VMEM((tiles, depth, tile), jnp.bfloat16),
            pltpu.VMEM((rows, 2, held, depth), jnp.bfloat16),
            pltpu.VMEM((units, held, tile), jnp.float32),
            pltpu.VMEM((units, held, tile), jnp.int16),
            pltpu.VMEM((units, 1, tile), jnp.float32),
            pltpu.VMEM((units, held, tile), jnp.int16),
            pltpu.VMEM((units, 1, tile), jnp.float32),
            pltpu.VMEM((tiles, 1, tile), jnp.float32),
            pltpu.VMEM((tiles, 1, tile), jnp.float32),
            dma((tiles,)),
            dma((2, 2, rows)),
            dma((2, rows)),
            dma((2, rows)),
            dma((2, rows)),
            dma((units,)),
            dma((units,)),
            dma((units,)),
            dma((units,)),
            dma,
            dma,
        ],
        compiler_params=pltpu.CompilerParams(
            collective_id=0, has_side_effects=True, vmem_limit_bytes=56 * 2**20
        ),
    )(tokens, up_weight, block_mask)
    return out.reshape(width)


def solution(mesh):
    placed = (
        P(("groups", "row", "tok"), "col"),
        P("col", ("row", "tok")),
        P("col", ("row", "tok")),
    )
    rows = mesh.shape["row"]
    pairs = mesh.shape["col"] == 2 and mesh.shape["tok"] == 2 and rows % 2 == 0 and rows > 2

    def body(tokens, up_weight, block_mask):
        held, depth = tokens.shape
        width = up_weight.shape[1]
        fits = up_weight.size * 2 <= VMEM_CAP and held % 16 == 0
        fits = fits and depth % (2 * BLOCK) == 0 and width % TILE == 0 and width > TILE
        if pairs and fits:
            return fused(rows, tokens, up_weight, block_mask)
        return per_device(tokens, up_weight, block_mask)

    return jax.shard_map(
        body,
        mesh=mesh,
        in_specs=placed,
        out_specs=P(("groups", "row", "tok")),
        check_vma=False,
    )
```
